32 devices in a mesh: groups: 2 (over x), tensor: 16 (over z, y, core).
Axes of the slice: x: 2, y: 2, z: 4, core: 2. Of those that a mesh axis runs over, the one named last changes fastest.
Arguments:
- tokens: bfloat16 [768, 4096], P(('groups', 'tensor')), parts along dimension 0, may hold values from -6 to 6
- targets: bfloat16 [768, 4096], P(('groups', 'tensor')), parts along dimension 0, may hold values from -6 to 6
- gate_weight: bfloat16 [4096, 16384], P(None, 'tensor'), may hold values from -0.09375 to 0.09375
- up_weight: bfloat16 [4096, 16384], P(None, 'tensor'), may hold values from -0.09375 to 0.09375
- down_weight: bfloat16 [16384, 4096], P('tensor'), may hold values from -0.046875 to 0.046875
- probe: bfloat16 [8192, 16384], P('groups', 'tensor'), parts along dimension 0, may hold values from -1 to 1, as said below
Outputs:
- hvp: bfloat16 [8192, 16384], P('groups', 'tensor'), parts along dimension 0
The draws below stay inside these ranges and needn't reach their ends.
There are 2 independent parts, one for each index of `groups`. The reference program is written for one: setup_inputs(seed, part) draws one part's arguments, and reference() takes and returns one part's arrays. A program takes and returns all parts, laid end to end along the dimension named above; an argument that names none is the same for every part. Nothing has to cross between parts.
Inputs may be any that keep to these rules, and one draw needn't show every extreme that they name: Every entry of the probe is -1 or 1.
All inputs are finite; a program needn't handle non-finite values.
Results may differ from the reference program's by a relative error of at most 0.006.
Values may be sent and summed in bfloat16 or wider, within the bound.
No kernel may reach another device: no remote copies, remote signals or barrier semaphores. Data moves between devices by JAX's collectives and lax.ppermute only.
A program may use at most 128 MiB of HBM per device.

```python
import jax
import jax.numpy as jnp

D = 4096
FF = 16384
TOKENS = 384


def draw_probe(key, part):
    key = jax.random.fold_in(key, 7)
    signs = jax.random.rademacher(key, (D, FF), dtype=jnp.float32)
    return signs.astype(jnp.bfloat16)


def steps_of(key, extent, shards, low, high):
    loudness = 1.0
    for axis_at, blocks in shards:
        draws = jax.random.uniform(jax.random.fold_in(jax.random.fold_in(key, 6), axis_at), (blocks,), jnp.float32, low / len(shards), high / len(shards))
        loudness = loudness * jnp.repeat(jnp.exp(draws), extent[axis_at] // blocks).reshape((-1,) + (1,) * (len(extent) - 1 - axis_at))
    return loudness


def scatter_about(own_key, extent, scale, bound, shards=(), kind=jnp.bfloat16):
    factor_of = steps_of(own_key, extent, shards, -0.22, 0.18) if shards else 1.0
    drawn = jax.random.normal(own_key, extent, jnp.float32) * scale * factor_of
    return jnp.minimum(jnp.maximum(drawn, -bound), bound).astype(kind)


def setup_inputs(seed: int = 0, part: int = 0) -> dict:
    streams_of = jax.random.split(jax.random.key(seed), 7)
    part_keys = jax.random.split(jax.random.fold_in(streams_of[6], part), 7)
    tokens = scatter_about(part_keys[0], (TOKENS, D), 1.0, 6.0, ((0, 16),))
    targets = scatter_about(part_keys[1], (TOKENS, D), 1.0, 6.0, ((0, 16),))
    gate_weight = scatter_about(streams_of[2], (D, FF), D ** -0.5, 0.09375, ((1, 16),))
    up_weight = scatter_about(streams_of[3], (D, FF), D ** -0.5, 0.09375, ((1, 16),))
    down_weight = scatter_about(streams_of[4], (FF, D), FF ** -0.5, 0.046875, ((0, 16),))
    probe = draw_probe(jax.random.fold_in(jax.random.fold_in(streams_of[6], part), 71), part)
    return {"tokens": tokens, "targets": targets, "gate_weight": gate_weight, "up_weight": up_weight, "down_weight": down_weight, "probe": probe}


def reference(tokens, targets, gate_weight, up_weight, down_weight, probe):
    count = tokens.shape[0]
    width = tokens.shape[1]
    preact = jnp.dot(tokens, gate_weight, preferred_element_type=jnp.float32)
    linear = jnp.dot(tokens, up_weight, preferred_element_type=jnp.float32)
    tangent = jnp.dot(tokens, probe, preferred_element_type=jnp.float32) * (width ** -0.5)
    logistic = jax.nn.sigmoid(preact)
    slopes = logistic * (1.0 + preact * (1.0 - logistic))
    curvature = logistic * (1.0 - logistic) * (2.0 + preact * (1.0 - 2.0 * logistic))
    hidden = (preact * logistic * linear).astype(jnp.bfloat16)
    hidden_dot = (slopes * tangent * linear).astype(jnp.bfloat16)
    output = jnp.dot(hidden, down_weight, preferred_element_type=jnp.float32)
    output_dot = jnp.dot(hidden_dot, down_weight, preferred_element_type=jnp.float32)
    errors = (output - targets.astype(jnp.float32)).astype(jnp.bfloat16)
    tangent_out = output_dot.astype(jnp.bfloat16)
    gradient = jnp.dot(errors, down_weight.T, preferred_element_type=jnp.float32)
    gradient_dot = jnp.dot(tangent_out, down_weight.T, preferred_element_type=jnp.float32)
    weighted = (gradient_dot * linear * slopes + gradient * linear * curvature * tangent).astype(jnp.bfloat16)
    result = jnp.dot(tokens.T, weighted, preferred_element_type=jnp.float32) * (count ** -0.5)
    return result.astype(jnp.bfloat16)
```

```python
import jax
import jax.numpy as jnp
from jax import lax
from jax.experimental import pallas as pl
from jax.experimental.pallas import tpu as pltpu
from jax.sharding import PartitionSpec as P

AXIS = "tensor"


def ring_routes(devices):
    chips = devices // 2
    cycle = list(range(0, chips, 2)) + list(range(1, chips, 2))[::-1]
    onward, backward = [], []
    for place, chip in enumerate(cycle):
        following = cycle[(place + 1) % chips]
        for core in range(2):
            onward.append((chip * 2 + core, following * 2 + core))
            backward.append((following * 2 + core, chip * 2 + core))
    partner = [(device, device ^ 1) for device in range(devices)]
    return onward, backward, partner


def send(block, route):
    return lax.ppermute(block, AXIS, route)


def gather_ring(own, devices):
    onward, backward, _ = ring_routes(devices)
    chips = devices // 2
    before, after = own, own
    blocks = [own]
    for _ in range((chips - 1) // 2):
        before, after = send(before, onward), send(after, backward)
        blocks += [before, after]
    if chips % 2 == 0:
        half = own.shape[-1] // 2
        blocks.append(
            jnp.concatenate(
                [send(before[..., :half], onward), send(after[..., half:], backward)], axis=-1
            )
        )
    return blocks


def scatter_ring(blocks, devices):
    onward, backward, _ = ring_routes(devices)
    chips = devices // 2
    steps = (chips - 1) // 2
    from_before = from_after = None
    if chips % 2 == 0:
        half = blocks[0].shape[-1] // 2
        far = blocks[-1].astype(jnp.bfloat16)
        from_before, from_after = send(far[..., :half], onward), send(far[..., half:], backward)
        rest = [(0, 0)] * (far.ndim - 1)
        from_before = jnp.pad(from_before.astype(jnp.float32), rest + [(0, half)])
        from_after = jnp.pad(from_after.astype(jnp.float32), rest + [(half, 0)])
    for distance in range(steps, 0, -1):
        to_after, to_before = blocks[2 * distance], blocks[2 * distance - 1]
        if from_before is not None:
            to_after, to_before = to_after + from_before, to_before + from_after
        from_before = send(to_after.astype(jnp.bfloat16), onward).astype(jnp.float32)
        from_after = send(to_before.astype(jnp.bfloat16), backward).astype(jnp.float32)
    return blocks[0] + from_before + from_after


def outer_kernel(scale, left_ref, right_ref, out_ref):
    product = jnp.dot(left_ref[...], right_ref[...], preferred_element_type=jnp.float32)
    out_ref[...] = (product * scale).astype(out_ref.dtype)


def outer(left, right, scale):
    rows, depth = left.shape
    columns = right.shape[1]
    tile = 512
    return pl.pallas_call(
        lambda *refs: outer_kernel(scale, *refs),
        grid=(rows // tile,),
        in_specs=[
            pl.BlockSpec((tile, depth), lambda i: (i, 0)),
            pl.BlockSpec((depth, columns), lambda i: (0, 0)),
        ],
        out_specs=pl.BlockSpec((tile, columns), lambda i: (i, 0)),
        out_shape=jax.ShapeDtypeStruct((rows, columns), jnp.bfloat16),
        compiler_params=pltpu.CompilerParams(vmem_limit_bytes=32 * 2**20),
        cost_estimate=pl.CostEstimate(
            flops=2 * rows * depth * columns,
            bytes_accessed=2 * (rows * depth + depth * columns + rows * columns),
            transcendentals=0,
        ),
        name="outer",
    )(left, right)


def on_device(devices, tokens, targets, gate_weight, up_weight, down_weight, probe):
    features = tokens.shape[1]
    mine = tokens.shape[0]
    partner = ring_routes(devices)[2]
    blocks = gather_ring(tokens, devices)
    count = len(blocks)
    near = max(1, min(5, count - 1))
    groups = [list(range(near)), list(range(near, count))]

    rows_of, saved, partial = [], [], [None] * count
    for group in groups:
        same = jnp.concatenate([blocks[b] for b in group])
        rows = jnp.concatenate([same, send(same, partner)])
        rows_of.append(rows)
        preact = jnp.dot(rows, gate_weight, preferred_element_type=jnp.float32)
        linear = jnp.dot(rows, up_weight, preferred_element_type=jnp.float32)
        tangent = jnp.dot(rows, probe, preferred_element_type=jnp.float32) * features ** (-0.5)
        logistic = jax.nn.sigmoid(preact)
        slopes = logistic * (1.0 + preact * (1.0 - logistic))
        curvature = logistic * (1.0 - logistic) * (2.0 + preact * (1.0 - 2.0 * logistic))
        hidden = (preact * logistic * linear).astype(jnp.bfloat16)
        hidden_dot = (slopes * tangent * linear).astype(jnp.bfloat16)
        saved.append((linear * slopes, linear * curvature * tangent))
        product = jnp.dot(
            jnp.concatenate([hidden, hidden_dot]), down_weight, preferred_element_type=jnp.float32
        ).reshape(2, 2, len(group), mine, features)
        summed = product[:, 0] + send(product[:, 1].astype(jnp.bfloat16), partner).astype(jnp.float32)
        for at, b in enumerate(group):
            partial[b] = summed[:, at]

    output, output_dot = scatter_ring(partial, devices)
    errors = (output - targets.astype(jnp.float32)).astype(jnp.bfloat16)
    stacked = jnp.stack([errors, output_dot.astype(jnp.bfloat16)])
    back = gather_ring(stacked, devices)

    weighted = []
    for group, (by_dot, by_error) in zip(groups, saved):
        same = jnp.concatenate([back[b] for b in group], axis=1)
        both = jnp.stack([same, send(same, partner)], axis=1)
        both = both.reshape(2, -1, features)
        gradient = lax.dot_general(
            both, down_weight, (((2,), (1,)), ((), ())), preferred_element_type=jnp.float32
        )
        weighted.append((gradient[1] * by_dot + gradient[0] * by_error).astype(jnp.bfloat16))
    everyone = jnp.concatenate(rows_of)
    return outer(everyone.T, jnp.concatenate(weighted), (mine * devices) ** (-0.5))


def solution(mesh):
    placed = (
        P(("groups", "tensor"), None),
        P(("groups", "tensor"), None),
        P(None, "tensor"),
        P(None, "tensor"),
        P("tensor", None),
        P("groups", "tensor"),
    )

    def whole(*arrays):
        return on_device(mesh.shape[AXIS], *arrays)

    return jax.shard_map(
        whole, mesh=mesh, in_specs=placed, out_specs=P("groups", "tensor"), check_vma=False
    )
```

```python
import functools

import jax
import jax.numpy as jnp
from jax import lax
from jax.experimental import pallas as pl
from jax.experimental.pallas import tpu as pltpu
from jax.sharding import PartitionSpec as P

AXIS = "tensor"
F32, BF16 = jnp.float32, jnp.bfloat16
MIB = 2**20
IN_VMEM = pl.BlockSpec(memory_space=pltpu.VMEM)
IN_SMEM = pl.BlockSpec(memory_space=pltpu.SMEM)


def ring_routes(devices):
    chips = devices // 2
    cycle = list(range(0, chips, 2)) + list(range(1, chips, 2))[::-1]
    onward, backward = [], []
    for place, chip in enumerate(cycle):
        following = cycle[(place + 1) % chips]
        for core in range(2):
            onward.append((chip * 2 + core, following * 2 + core))
            backward.append((following * 2 + core, chip * 2 + core))
    partner = [(device, device ^ 1) for device in range(devices)]
    return onward, backward, partner


def send(block, route):
    return lax.ppermute(block, AXIS, route)


def tie(*arrays):
    return lax.optimization_barrier(arrays)


def call(kernel, name, core, outs, scratch, flops, operands, from_hbm=()):
    limit = 6 * MIB + sum(4 * shape[0] * shape[1] for shape in scratch)
    semaphores = [pltpu.SemaphoreType.DMA((1,))] if from_hbm else []
    return pl.pallas_call(
        kernel,
        in_specs=[IN_SMEM]
        + [IN_VMEM] * len(operands)
        + [pl.BlockSpec(memory_space=pltpu.HBM)] * len(from_hbm),
        out_specs=[IN_VMEM] * len(outs),
        out_shape=[pltpu.VMEM(shape, kind) for shape, kind in outs],
        scratch_shapes=[pltpu.VMEM(shape, F32) for shape in scratch] + semaphores,
        compiler_params=pltpu.CompilerParams(vmem_limit_bytes=limit),
        cost_estimate=pl.CostEstimate(
            flops=flops, bytes_accessed=sum(x.size * 2 for x in operands), transcendentals=0
        ),
        name=name,
    )(core, *[in_vmem(x) for x in operands], *[in_hbm(x) for x in from_hbm])


def in_hbm(x):
    return pltpu.with_memory_space_constraint(x, pltpu.HBM)


def in_vmem(x):
    return pltpu.with_memory_space_constraint(x, pltpu.VMEM)


def fetch(weights, after):
    count = len(weights)

    def kernel(after_ref, *refs):
        copies = [
            pltpu.make_async_copy(refs[i], refs[count + i], refs[-1].at[i]) for i in range(count)
        ]
        for copy in copies:
            copy.start()
        for copy in copies:
            copy.wait()

    return pl.pallas_call(
        kernel,
        in_specs=[pl.BlockSpec(memory_space=pl.ANY)] + [pl.BlockSpec(memory_space=pltpu.HBM)] * count,
        out_specs=[IN_VMEM] * count,
        out_shape=[pltpu.VMEM(w.shape, w.dtype) for w in weights],
        scratch_shapes=[pltpu.SemaphoreType.DMA((count,))],
        compiler_params=pltpu.CompilerParams(vmem_limit_bytes=MIB),
        cost_estimate=pl.CostEstimate(
            flops=0, bytes_accessed=sum(2 * w.size for w in weights), transcendentals=0
        ),
        name="fetch",
    )(after, *[in_hbm(w) for w in weights])


def passes(core, half, tile):
    for own in (True, False):
        start = (core if own else 1 - core) * half
        for k in range(0, half, tile):
            yield own, slice(k, k + tile), pl.ds(pl.multiple_of(start + k, tile), tile)


def forward(core, same, other, weights, late=None, beside=None):
    count, rows = len(same), same[0].shape[0]
    total = count * rows
    depth, columns = weights[0].shape
    known = len(weights)
    coming = [w for w in (late, beside) if w is not None]

    def kernel(core_ref, *refs):
        blocks, refs = refs[: 2 * count], refs[2 * count :]
        weight_refs, refs = list(refs[:known]), refs[known:]
        source, refs = refs[: len(coming)], refs[len(coming) :]
        (hidden_ref, by_dot_ref, by_error_ref), refs = refs[:3], refs[3:]
        arriving, refs = refs[: len(coming)], refs[len(coming) :]
        sums = refs[:3]
        if coming:
            copy = pltpu.make_async_copy(source[0], arriving[0], refs[3].at[0])
            copy.start()
            if late is not None:
                weight_refs.append(arriving[0])

        def add(some):
            for own, near, at in passes(core_ref[0], depth // 2, 1024):
                part = blocks[:count] if own else blocks[count:]
                left = jnp.concatenate([b[:, near] for b in part])
                for s, w in some:
                    product = jnp.dot(left, w[at, :], preferred_element_type=F32)
                    if own and near.start == 0:
                        s[...] = product
                    else:
                        s[...] += product

        pairs = list(zip(sums, weight_refs))
        add(pairs[:known])
        if coming:
            copy.wait()
        if late is not None:
            add(pairs[known:])
        for b in range(count):
            at = slice(b * rows, (b + 1) * rows)
            preact, linear = sums[0][at, :], sums[1][at, :]
            tangent = sums[2][at, :] * depth ** (-0.5)
            logistic = jax.nn.sigmoid(preact)
            slopes = logistic * (1.0 + preact * (1.0 - logistic))
            curvature = logistic * (1.0 - logistic) * (2.0 + preact * (1.0 - 2.0 * logistic))
            by_dot = linear * slopes
            by_dot_ref[at, :] = by_dot
            by_error_ref[at, :] = linear * curvature * tangent
            hidden_ref[2 * b * rows : (2 * b + 1) * rows, :] = (preact * logistic * linear).astype(BF16)
            hidden_ref[(2 * b + 1) * rows : (2 * b + 2) * rows, :] = (by_dot * tangent).astype(BF16)

    return call(
        kernel,
        "forward",
        core,
        [((2 * total, columns), BF16), ((total, columns), F32), ((total, columns), F32)]
        + [(w.shape, w.dtype) for w in coming],
        [(total, columns)] * 3,
        6 * total * depth * columns,
        [*same, *other, *weights],
        coming,
    )


def down(core, hidden, down_weight, both=True, own_half=True):
    total = sum(h.shape[0] for h in hidden)
    depth, columns = down_weight.shape
    half = columns // 2
    places = 2 if both else 1

    def kernel(core_ref, *refs):
        hidden_refs, weight_ref, out_refs = refs[: len(hidden)], refs[len(hidden)], refs[len(hidden) + 1 :]
        left = jnp.concatenate([h[...] for h in hidden_refs])
        first = core_ref[0] if own_half and not both else 1 - core_ref[0]
        for mine, near, at in passes(first, half, 1024):
            if mine or both:
                product = jnp.dot(left, weight_ref[:, at], preferred_element_type=F32)
                out_refs[0 if mine else 1][:, near] = product.astype(BF16)

    return call(
        kernel,
        "down",
        core,
        [((total, half), BF16)] * places,
        [],
        places * total * depth * columns,
        [*hidden, down_weight],
    )


def back(core, same, other, down_weight, by_dot, by_error):
    count, rows = len(same), same[0].shape[0]
    total = count * rows
    columns, depth = down_weight.shape
    parts = len(by_dot)

    def kernel(core_ref, *refs):
        blocks, refs = refs[: 2 * count], refs[2 * count :]
        weight_ref, by_dot_refs, by_error_refs = refs[0], refs[1 : 1 + parts], refs[1 + parts : -2]
        out_ref, sum_ref = refs[-2:]
        for own, near, at in passes(core_ref[0], depth // 2, 1024):
            left = jnp.concatenate([b[:, near] for b in (blocks[:count] if own else blocks[count:])])
            product = lax.dot_general(
                left, weight_ref[:, at], (((1,), (1,)), ((), ())), preferred_element_type=F32
            )
            if own and near.start == 0:
                sum_ref[...] = product
            else:
                sum_ref[...] += product
        half = rows // 2
        b = 0
        for by_dot_ref, by_error_ref in zip(by_dot_refs, by_error_refs):
            for start in range(0, by_dot_ref.shape[0], half):
                at = slice(start, start + half)
                gradient = sum_ref[b * rows : b * rows + half, :]
                gradient_dot = sum_ref[b * rows + half : (b + 1) * rows, :]
                out_ref[b * half : (b + 1) * half, :] = (
                    gradient_dot * by_dot_ref[at, :] + gradient * by_error_ref[at, :]
                ).astype(BF16)
                b += 1

    return call(
        kernel,
        "back",
        core,
        [((total // 2, columns), BF16)],
        [(total, columns)],
        2 * total * depth * columns,
        [*same, *other, down_weight, *by_dot, *by_error],
    )[0]


def outer(core, same, other, weighted, scale):
    count, rows = len(same), same[0].shape[0]
    half = same[0].shape[1]
    total, depth = count * rows, 2 * half
    columns = weighted[0].shape[1]
    tile = 512

    def kernel(core_ref, *refs):
        blocks, refs = refs[: 2 * count], refs[2 * count :]
        weighted_refs, (out_ref, held, sems) = refs[:-3], refs[-3:]
        right = jnp.concatenate([w[...] for w in weighted_refs])
        copies = []
        for own, near, at in passes(core_ref[0], half, tile):
            left = jnp.concatenate([b[:, near] for b in (blocks[:count] if own else blocks[count:])])
            product = lax.dot_general(
                left, right, (((0,), (0,)), ((), ())), preferred_element_type=F32
            )
            slot = len(copies)
            held[slot] = (product * scale).astype(BF16)
            copies.append(pltpu.make_async_copy(held.at[slot], out_ref.at[at], sems.at[slot]))
            copies[-1].start()
        for copy in copies:
            copy.wait()

    operands = [*same, *other, *weighted]
    tiles = depth // tile
    return pl.pallas_call(
        kernel,
        in_specs=[IN_SMEM] + [IN_VMEM] * len(operands),
        out_specs=pl.BlockSpec(memory_space=pltpu.HBM),
        out_shape=jax.ShapeDtypeStruct((depth, columns), BF16),
        scratch_shapes=[pltpu.VMEM((tiles, tile, columns), BF16), pltpu.SemaphoreType.DMA((tiles,))],
        compiler_params=pltpu.CompilerParams(vmem_limit_bytes=24 * MIB),
        cost_estimate=pl.CostEstimate(
            flops=2 * total * depth * columns, bytes_accessed=2 * depth * columns, transcendentals=0
        ),
        name="outer",
    )(core, *[in_vmem(x) for x in operands])


def on_device(devices, tokens, targets, gate_weight, up_weight, down_weight, probe):
    mine, features = tokens.shape
    rows, half, quarter = 2 * mine, features // 2, features // 4
    onward, backward, partner = ring_routes(devices)
    chips = devices // 2
    steps = (chips - 1) // 2
    count = chips
    even = chips % 2 == 0
    index = lax.rem(lax.axis_index(AXIS), 2)
    core = index.astype(jnp.int32).reshape(1)

    def chip_rows(array):
        keep = lax.dynamic_slice(array, (0, index * half), (mine, half))
        give = lax.dynamic_slice(array, (0, (1 - index) * half), (mine, half))
        got = send(give, partner)
        return jnp.where(index == 0, jnp.concatenate([keep, got]), jnp.concatenate([got, keep]))

    last = 1 + 2 * steps
    cuts = [0, max(1, last - 4), max(1, last - 2), count]
    groups = [list(range(a, b)) for a, b in zip(cuts, cuts[1:]) if a < b]

    def gather(owns, work):
        chains = range(len(owns))
        same, other = [[own] for own in owns], [[] for _ in owns]
        ends = [(own, own) for own in owns]

        def swap():
            for c in chains:
                other[c] += [send(block, partner) for block in same[c][len(other[c]) :]]

        for step in range(1, steps + 1):
            moved = [(send(ends[c][0], onward), send(ends[c][1], backward)) for c in chains]
            swap()
            done = work(step, same, other)
            for c in chains:
                before, after, *_ = tie(*moved[c], *(done if c == 0 else ()))
                ends[c] = before, after
                same[c] += [before, after]
        if even:
            moved = [
                (send(ends[c][0][:, :quarter], onward), send(ends[c][1][:, quarter:], backward))
                for c in chains
            ]
            swap()
            done = work(steps + 1, same, other)
            for c in chains:
                near, far, *_ = tie(*moved[c], *(done if c == 0 else ()))
                same[c].append(jnp.concatenate([near, far], axis=1))
        swap()
        work(steps + 2, same, other)
        return same, other

    hidden, by_dot, by_error = [], [], []
    weights = {}

    def run_forward(step, same, other):
        same, other = same[0], other[0]
        if step == 1:
            weights["gate"], weights["up"] = fetch([gate_weight, up_weight], same[0])
            return [weights["gate"], weights["up"]]
        done = []
        ready = len(other) if step > steps + 1 else len(other) - 2
        while len(hidden) < len(groups) and groups[len(hidden)][-1] < ready:
            g = groups[len(hidden)]
            at = slice(g[0], g[-1] + 1)
            late = None if "probe" in weights else probe
            beside = down_weight if late is None and "down" not in weights else None
            known = [weights[n] for n in ("gate", "up", "probe") if n in weights]
            h, d, e, *came = forward(core, same[at], other[at], known, late, beside)
            hidden.append(h), by_dot.append(d), by_error.append(e)
            if came:
                weights["down" if late is None else "probe"] = came[0]
            done.append(h)
            if step <= steps + 1:
                break
        return done

    (same,), (other,) = gather([chip_rows(tokens)], run_forward)
    if "down" not in weights:
        (weights["down"],) = fetch([down_weight], hidden[-1])
    goals = chip_rows(targets).astype(F32)

    split = max(len(groups) - 1, 1)
    near_blocks = [b for g in groups[:split] for b in g]
    far_blocks = [b for g in groups[split:] for b in g]
    partial, swapped = {}, {}

    def keep(blocks, own, others):
        for at, b in enumerate(blocks):
            at = slice(2 * rows * at, 2 * rows * (at + 1))
            partial[b] = own[at]
            swapped[b] = send(others[at], partner)

    def block_of(b):
        return partial[b].astype(F32) + swapped[b].astype(F32)

    def near_work(after):
        hidden_near = tie(*hidden[:split], after)[:-1]
        others, own = down(core, hidden_near, weights["down"])
        keep(near_blocks, own, others)
        return own

    if far_blocks:
        (others,) = down(core, hidden[split:], weights["down"], both=False, own_half=False)
        (own,) = down(core, [*hidden[split:]], weights["down"], both=False)
        keep(far_blocks, own, others)
    else:
        near_work(hidden[-1])

    from_before = from_after = None
    if even:
        far = block_of(count - 1).astype(BF16)
        from_before, from_after = send(far[:, :quarter], onward), send(far[:, quarter:], backward)
        if far_blocks:
            from_before, from_after, _ = tie(from_before, from_after, near_work(far))
        from_before = jnp.pad(from_before.astype(F32), [(0, 0), (0, quarter)])
        from_after = jnp.pad(from_after.astype(F32), [(0, 0), (quarter, 0)])
    for distance in range(steps, 0, -1):
        to_after, to_before = block_of(2 * distance), block_of(2 * distance - 1)
        if from_before is not None:
            to_after, to_before = to_after + from_before, to_before + from_after
        to_after, to_before = tie(to_after.astype(BF16), to_before.astype(BF16))
        from_before, from_after = send(to_after, onward), send(to_before, backward)
        if distance == steps and not even and far_blocks:
            from_before, from_after, _ = tie(from_before, from_after, near_work(to_after))
        from_before, from_after = tie(from_before, from_after)
        from_before, from_after = from_before.astype(F32), from_after.astype(F32)
    total = block_of(0) + from_before + from_after
    message = jnp.concatenate([total[:rows] - goals, total[rows:]]).astype(BF16)

    weighted = []
    back_groups = [groups[:split], *[[g] for g in groups[split:]]]

    def run_back(step, same, other):
        done = []
        ready = len(other[0])
        while len(weighted) < len(back_groups) and back_groups[len(weighted)][-1][-1] < ready:
            gs = back_groups[len(weighted)]
            at = slice(gs[0][0], gs[-1][-1] + 1)
            first = sum(len(x) for x in back_groups[: len(weighted)])
            saved = slice(first, first + len(gs))
            weighted.append(
                back(
                    core,
                    same[0][at],
                    other[0][at],
                    weights["down"],
                    by_dot[saved],
                    by_error[saved],
                )
            )
            done.append(weighted[-1])
        return done

    gather([message], run_back)
    return outer(core, same, other, weighted, (mine * devices) ** (-0.5))


def solution(mesh):
    placed = (
        P(("groups", "tensor"), None),
        P(("groups", "tensor"), None),
        P(None, "tensor"),
        P(None, "tensor"),
        P("tensor", None),
        P("groups", "tensor"),
    )
    return jax.shard_map(
        functools.partial(on_device, mesh.shape[AXIS]),
        mesh=mesh,
        in_specs=placed,
        out_specs=P("groups", "tensor"),
        check_vma=False,
    )
```

```python
import functools

import jax
import jax.numpy as jnp
from jax import lax
from jax.experimental import pallas as pl
from jax.experimental.pallas import tpu as pltpu
from jax.sharding import PartitionSpec as P

AXIS = "tensor"
F32, BF16 = jnp.float32, jnp.bfloat16
MIB = 2**20
IN_VMEM = pl.BlockSpec(memory_space=pltpu.VMEM)
IN_SMEM = pl.BlockSpec(memory_space=pltpu.SMEM)


def ring_routes(devices):
    chips = devices // 2
    cycle = list(range(0, chips, 2)) + list(range(1, chips, 2))[::-1]
    onward, backward = [], []
    for place, chip in enumerate(cycle):
        following = cycle[(place + 1) % chips]
        for core in range(2):
            onward.append((chip * 2 + core, following * 2 + core))
            backward.append((following * 2 + core, chip * 2 + core))
    partner = [(device, device ^ 1) for device in range(devices)]
    return onward, backward, partner


def send(block, route):
    return lax.ppermute(block, AXIS, route)


def tie(*arrays):
    return lax.optimization_barrier(arrays)


def call(kernel, name, core, outs, scratch, flops, operands, from_hbm=()):
    limit = 6 * MIB + sum(4 * shape[0] * shape[1] for shape in scratch)
    semaphores = [pltpu.SemaphoreType.DMA((1,))] if from_hbm else []
    return pl.pallas_call(
        kernel,
        in_specs=[IN_SMEM]
        + [IN_VMEM] * len(operands)
        + [pl.BlockSpec(memory_space=pltpu.HBM)] * len(from_hbm),
        out_specs=[IN_VMEM] * len(outs),
        out_shape=[pltpu.VMEM(shape, kind) for shape, kind in outs],
        scratch_shapes=[pltpu.VMEM(shape, F32) for shape in scratch] + semaphores,
        compiler_params=pltpu.CompilerParams(vmem_limit_bytes=limit),
        cost_estimate=pl.CostEstimate(
            flops=flops, bytes_accessed=sum(x.size * 2 for x in operands), transcendentals=0
        ),
        name=name,
    )(core, *[in_vmem(x) for x in operands], *[in_hbm(x) for x in from_hbm])


def in_hbm(x):
    return pltpu.with_memory_space_constraint(x, pltpu.HBM)


def in_vmem(x):
    return pltpu.with_memory_space_constraint(x, pltpu.VMEM)


def fetch(weights, after):
    count = len(weights)

    def kernel(after_ref, *refs):
        copies = [
            pltpu.make_async_copy(refs[i], refs[count + i], refs[-1].at[i]) for i in range(count)
        ]
        for copy in copies:
            copy.start()
        for copy in copies:
            copy.wait()

    return pl.pallas_call(
        kernel,
        in_specs=[pl.BlockSpec(memory_space=pl.ANY)] + [pl.BlockSpec(memory_space=pltpu.HBM)] * count,
        out_specs=[IN_VMEM] * count,
        out_shape=[pltpu.VMEM(w.shape, w.dtype) for w in weights],
        scratch_shapes=[pltpu.SemaphoreType.DMA((count,))],
        compiler_params=pltpu.CompilerParams(vmem_limit_bytes=MIB),
        cost_estimate=pl.CostEstimate(
            flops=0, bytes_accessed=sum(2 * w.size for w in weights), transcendentals=0
        ),
        name="fetch",
    )(after, *[in_hbm(w) for w in weights])


def passes(core, half, tile):
    for own in (True, False):
        start = (core if own else 1 - core) * half
        for k in range(0, half, tile):
            yield own, slice(k, k + tile), pl.ds(pl.multiple_of(start + k, tile), tile)


def forward_own(core, same, weights):
    count = len(same)
    total = sum(b.shape[0] for b in same)
    depth, columns = weights[0].shape

    def kernel(core_ref, *refs):
        blocks, weight_refs, sums = refs[:count], refs[count : count + 3], refs[count + 3 :]
        for own, near, at in passes(core_ref[0], depth // 2, 1024):
            if own:
                left = jnp.concatenate([b[:, near] for b in blocks])
                for s, w in zip(sums, weight_refs):
                    product = jnp.dot(left, w[at, :], preferred_element_type=F32)
                    if near.start == 0:
                        s[...] = product
                    else:
                        s[...] += product

    return call(
        kernel,
        "forward_own",
        core,
        [((total, columns), F32)] * 3,
        [],
        3 * total * depth * columns,
        [*same, *weights],
    )


def forward(core, same, other, weights, late=None, beside=None, begun=()):
    count, rows = len(other), other[0].shape[0]
    same = [] if begun else same
    first = len(same)
    total = count * rows
    depth, columns = weights[0].shape
    known = len(weights)
    coming = [w for w in (late, beside) if w is not None]

    def kernel(core_ref, *refs):
        blocks, refs = refs[: first + count], refs[first + count :]
        weight_refs, refs = list(refs[:known]), refs[known:]
        begun_refs, refs = refs[: len(begun)], refs[len(begun) :]
        source, refs = refs[: len(coming)], refs[len(coming) :]
        (hidden_ref, by_dot_ref, by_error_ref), refs = refs[:3], refs[3:]
        arriving, refs = refs[: len(coming)], refs[len(coming) :]
        sums = refs[:3]
        if coming:
            copy = pltpu.make_async_copy(source[0], arriving[0], refs[3].at[0])
            copy.start()
            if late is not None:
                weight_refs.append(arriving[0])

        def add(some):
            for own, near, at in passes(core_ref[0], depth // 2, 1024):
                part = blocks[:first] if own else blocks[first:]
                if not part:
                    continue
                left = jnp.concatenate([b[:, near] for b in part])
                for n, (s, w) in enumerate(some):
                    product = jnp.dot(left, w[at, :], preferred_element_type=F32)
                    if begun and near.start == 0:
                        s[...] = begun_refs[n][...] + product
                    elif own and near.start == 0:
                        s[...] = product
                    else:
                        s[...] += product

        pairs = list(zip(sums, weight_refs))
        add(pairs[:known])
        if coming:
            copy.wait()
        if late is not None:
            add(pairs[known:])
        for b in range(count):
            at = slice(b * rows, (b + 1) * rows)
            preact, linear = sums[0][at, :], sums[1][at, :]
            tangent = sums[2][at, :] * depth ** (-0.5)
            logistic = jax.nn.sigmoid(preact)
            slopes = logistic * (1.0 + preact * (1.0 - logistic))
            curvature = logistic * (1.0 - logistic) * (2.0 + preact * (1.0 - 2.0 * logistic))
            by_dot = linear * slopes
            by_dot_ref[at, :] = by_dot
            by_error_ref[at, :] = linear * curvature * tangent
            hidden_ref[2 * b * rows : (2 * b + 1) * rows, :] = (preact * logistic * linear).astype(BF16)
            hidden_ref[(2 * b + 1) * rows : (2 * b + 2) * rows, :] = (by_dot * tangent).astype(BF16)

    return call(
        kernel,
        "forward",
        core,
        [((2 * total, columns), BF16), ((total, columns), F32), ((total, columns), F32)]
        + [(w.shape, w.dtype) for w in coming],
        [(total, columns)] * 3,
        (3 if begun else 6) * total * depth * columns,
        [*same, *other, *weights, *begun],
        coming,
    )


def down(core, hidden, down_weight, both=True, own_half=True):
    total = sum(h.shape[0] for h in hidden)
    depth, columns = down_weight.shape
    half = columns // 2
    places = 2 if both else 1

    def kernel(core_ref, *refs):
        hidden_refs, weight_ref, out_refs = refs[: len(hidden)], refs[len(hidden)], refs[len(hidden) + 1 :]
        left = jnp.concatenate([h[...] for h in hidden_refs])
        first = core_ref[0] if own_half and not both else 1 - core_ref[0]
        for mine, near, at in passes(first, half, 1024):
            if mine or both:
                product = jnp.dot(left, weight_ref[:, at], preferred_element_type=F32)
                out_refs[0 if mine else 1][:, near] = product.astype(BF16)

    return call(
        kernel,
        "down",
        core,
        [((total, half), BF16)] * places,
        [],
        places * total * depth * columns,
        [*hidden, down_weight],
    )


def back_own(core, same, down_weight):
    total = sum(b.shape[0] for b in same)
    columns, depth = down_weight.shape

    def kernel(core_ref, *refs):
        blocks, weight_ref, sum_ref = refs[:-2], refs[-2], refs[-1]
        for own, near, at in passes(core_ref[0], depth // 2, 1024):
            if own:
                left = jnp.concatenate([b[:, near] for b in blocks])
                product = lax.dot_general(
                    left, weight_ref[:, at], (((1,), (1,)), ((), ())), preferred_element_type=F32
                )
                if near.start == 0:
                    sum_ref[...] = product
                else:
                    sum_ref[...] += product

    return call(
        kernel,
        "back_own",
        core,
        [((total, columns), F32)],
        [],
        total * depth * columns,
        [*same, down_weight],
    )


def back(core, same, other, down_weight, by_dot, by_error, begun=()):
    count, rows = len(other), other[0].shape[0]
    total = count * rows
    same = [] if begun else same
    first = len(same)
    columns, depth = down_weight.shape
    parts = len(by_dot)

    def kernel(core_ref, *refs):
        blocks, refs = refs[: first + count], refs[first + count :]
        begun_refs, refs = refs[: len(begun)], refs[len(begun) :]
        weight_ref, by_dot_refs, by_error_refs = refs[0], refs[1 : 1 + parts], refs[1 + parts : -2]
        out_ref, sum_ref = refs[-2:]
        for own, near, at in passes(core_ref[0], depth // 2, 1024):
            part = blocks[:first] if own else blocks[first:]
            if not part:
                continue
            left = jnp.concatenate([b[:, near] for b in part])
            product = lax.dot_general(
                left, weight_ref[:, at], (((1,), (1,)), ((), ())), preferred_element_type=F32
            )
            if begun and near.start == 0:
                sum_ref[...] = begun_refs[0][...] + product
            elif own and near.start == 0:
                sum_ref[...] = product
            else:
                sum_ref[...] += product
        half = rows // 2
        b = 0
        for by_dot_ref, by_error_ref in zip(by_dot_refs, by_error_refs):
            for start in range(0, by_dot_ref.shape[0], half):
                at = slice(start, start + half)
                gradient = sum_ref[b * rows : b * rows + half, :]
                gradient_dot = sum_ref[b * rows + half : (b + 1) * rows, :]
                out_ref[b * half : (b + 1) * half, :] = (
                    gradient_dot * by_dot_ref[at, :] + gradient * by_error_ref[at, :]
                ).astype(BF16)
                b += 1

    return call(
        kernel,
        "back",
        core,
        [((total // 2, columns), BF16)],
        [(total, columns)],
        (1 if begun else 2) * total * depth * columns,
        [*same, *other, *begun, down_weight, *by_dot, *by_error],
    )[0]


def outer(core, same, other, weighted, scale):
    count, rows = len(same), same[0].shape[0]
    half = same[0].shape[1]
    total, depth = count * rows, 2 * half
    columns = weighted[0].shape[1]
    tile = 512

    def kernel(core_ref, *refs):
        blocks, refs = refs[: 2 * count], refs[2 * count :]
        weighted_refs, (out_ref, held, sems) = refs[:-3], refs[-3:]
        right = jnp.concatenate([w[...] for w in weighted_refs])
        copies = []
        for own, near, at in passes(core_ref[0], half, tile):
            left = jnp.concatenate([b[:, near] for b in (blocks[:count] if own else blocks[count:])])
            product = lax.dot_general(
                left, right, (((0,), (0,)), ((), ())), preferred_element_type=F32
            )
            slot = len(copies)
            held[slot] = (product * scale).astype(BF16)
            copies.append(pltpu.make_async_copy(held.at[slot], out_ref.at[at], sems.at[slot]))
            copies[-1].start()
        for copy in copies:
            copy.wait()

    operands = [*same, *other, *weighted]
    tiles = depth // tile
    return pl.pallas_call(
        kernel,
        in_specs=[IN_SMEM] + [IN_VMEM] * len(operands),
        out_specs=pl.BlockSpec(memory_space=pltpu.HBM),
        out_shape=jax.ShapeDtypeStruct((depth, columns), BF16),
        scratch_shapes=[pltpu.VMEM((tiles, tile, columns), BF16), pltpu.SemaphoreType.DMA((tiles,))],
        compiler_params=pltpu.CompilerParams(vmem_limit_bytes=24 * MIB),
        cost_estimate=pl.CostEstimate(
            flops=2 * total * depth * columns, bytes_accessed=2 * depth * columns, transcendentals=0
        ),
        name="outer",
    )(core, *[in_vmem(x) for x in operands])


def on_device(devices, tokens, targets, gate_weight, up_weight, down_weight, probe):
    mine, features = tokens.shape
    rows, half, quarter = 2 * mine, features // 2, features // 4
    onward, backward, partner = ring_routes(devices)
    chips = devices // 2
    steps = (chips - 1) // 2
    count = chips
    even = chips % 2 == 0
    index = lax.rem(lax.axis_index(AXIS), 2)
    core = index.astype(jnp.int32).reshape(1)

    def chip_rows(array):
        keep = lax.dynamic_slice(array, (0, index * half), (mine, half))
        give = lax.dynamic_slice(array, (0, (1 - index) * half), (mine, half))
        got = send(give, partner)
        return jnp.where(index == 0, jnp.concatenate([keep, got]), jnp.concatenate([got, keep]))

    last = 1 + 2 * steps
    cuts = [0, max(1, last - 4), max(1, last - 2), count]
    groups = [list(range(a, b)) for a, b in zip(cuts, cuts[1:]) if a < b]

    def gather(owns, work):
        chains = range(len(owns))
        same, other = [[own] for own in owns], [[] for _ in owns]
        ends = [(own, own) for own in owns]

        def swap():
            for c in chains:
                other[c] += [send(block, partner) for block in same[c][len(other[c]) :]]

        for step in range(1, steps + 1):
            moved = [(send(ends[c][0], onward), send(ends[c][1], backward)) for c in chains]
            swap()
            done = work(step, same, other)
            for c in chains:
                before, after, *_ = tie(*moved[c], *(done if c == 0 else ()))
                ends[c] = before, after
                same[c] += [before, after]
        if even:
            moved = [
                (send(ends[c][0][:, :quarter], onward), send(ends[c][1][:, quarter:], backward))
                for c in chains
            ]
            swap()
            done = work(steps + 1, same, other)
            for c in chains:
                near, far, *_ = tie(*moved[c], *(done if c == 0 else ()))
                same[c].append(jnp.concatenate([near, far], axis=1))
        swap()
        work(steps + 2, same, other)
        return same, other

    hidden, by_dot, by_error = [], [], []
    weights = {}

    def run_forward(step, same, other):
        same, other = same[0], other[0]
        if step == 1:
            weights["gate"], weights["up"] = fetch([gate_weight, up_weight], same[0])
            return [weights["gate"], weights["up"]]
        done = []
        ready = len(other) if step > steps + 1 else len(other) - 2
        while len(hidden) < len(groups) and groups[len(hidden)][-1] < ready:
            g = groups[len(hidden)]
            at = slice(g[0], g[-1] + 1)
            late = None if "probe" in weights else probe
            beside = down_weight if late is None and "down" not in weights else None
            known = [weights[n] for n in ("gate", "up", "probe") if n in weights]
            begun = ()
            if step > steps + 1 and late is None:
                begun = forward_own(core, same[at], known)
            h, d, e, *came = forward(core, same[at], other[at], known, late, beside, begun)
            hidden.append(h), by_dot.append(d), by_error.append(e)
            if came:
                weights["down" if late is None else "probe"] = came[0]
            done.append(h)
            if step <= steps + 1:
                break
        return done

    (same,), (other,) = gather([chip_rows(tokens)], run_forward)
    if "down" not in weights:
        (weights["down"],) = fetch([down_weight], hidden[-1])
    goals = chip_rows(targets).astype(F32)

    split = max(len(groups) - 1, 1)
    near_blocks = [b for g in groups[:split] for b in g]
    far_blocks = [b for g in groups[split:] for b in g]
    partial, swapped = {}, {}

    def keep(blocks, own, others):
        for at, b in enumerate(blocks):
            at = slice(2 * rows * at, 2 * rows * (at + 1))
            partial[b] = own[at]
            swapped[b] = send(others[at], partner)

    def block_of(b):
        return partial[b].astype(F32) + swapped[b].astype(F32)

    def near_work(after):
        hidden_near = tie(*hidden[:split], after)[:-1]
        others, own = down(core, hidden_near, weights["down"])
        keep(near_blocks, own, others)
        return own

    if far_blocks:
        (others,) = down(core, hidden[split:], weights["down"], both=False, own_half=False)
        (own,) = down(core, [*hidden[split:]], weights["down"], both=False)
        keep(far_blocks, own, others)
    else:
        near_work(hidden[-1])

    from_before = from_after = None
    if even:
        far = block_of(count - 1).astype(BF16)
        from_before, from_after = send(far[:, :quarter], onward), send(far[:, quarter:], backward)
        if far_blocks:
            from_before, from_after, _ = tie(from_before, from_after, near_work(far))
        from_before = jnp.pad(from_before.astype(F32), [(0, 0), (0, quarter)])
        from_after = jnp.pad(from_after.astype(F32), [(0, 0), (quarter, 0)])
    for distance in range(steps, 0, -1):
        to_after, to_before = block_of(2 * distance), block_of(2 * distance - 1)
        if from_before is not None:
            to_after, to_before = to_after + from_before, to_before + from_after
        to_after, to_before = tie(to_after.astype(BF16), to_before.astype(BF16))
        from_before, from_after = send(to_after, onward), send(to_before, backward)
        if distance == steps and not even and far_blocks:
            from_before, from_after, _ = tie(from_before, from_after, near_work(to_after))
        from_before, from_after = tie(from_before, from_after)
        from_before, from_after = from_before.astype(F32), from_after.astype(F32)
    total = block_of(0) + from_before + from_after
    message = jnp.concatenate([total[:rows] - goals, total[rows:]]).astype(BF16)

    weighted = []
    back_groups = [groups[:split], *[[g] for g in groups[split:]]]

    def run_back(step, same, other):
        done = []
        ready = len(other[0])
        while len(weighted) < len(back_groups) and back_groups[len(weighted)][-1][-1] < ready:
            gs = back_groups[len(weighted)]
            at = slice(gs[0][0], gs[-1][-1] + 1)
            first = sum(len(x) for x in back_groups[: len(weighted)])
            saved = slice(first, first + len(gs))
            begun = back_own(core, same[0][at], weights["down"]) if step > steps + 1 else ()
            weighted.append(
                back(
                    core,
                    same[0][at],
                    other[0][at],
                    weights["down"],
                    by_dot[saved],
                    by_error[saved],
                    begun,
                )
            )
            done.append(weighted[-1])
        return done

    gather([message], run_back)
    return outer(core, same, other, weighted, (mine * devices) ** (-0.5))


def solution(mesh):
    placed = (
        P(("groups", "tensor"), None),
        P(("groups", "tensor"), None),
        P(None, "tensor"),
        P(None, "tensor"),
        P("tensor", None),
        P("groups", "tensor"),
    )
    return jax.shard_map(
        functools.partial(on_device, mesh.shape[AXIS]),
        mesh=mesh,
        in_specs=placed,
        out_specs=P("groups", "tensor"),
        check_vma=False,
    )
```

```python
import functools

import jax
import jax.numpy as jnp
from jax import lax
from jax.experimental import pallas as pl
from jax.experimental.pallas import tpu as pltpu
from jax.sharding import PartitionSpec as P

AXIS = "tensor"
F32, BF16 = jnp.float32, jnp.bfloat16
MIB = 2**20
IN_VMEM = pl.BlockSpec(memory_space=pltpu.VMEM)
IN_SMEM = pl.BlockSpec(memory_space=pltpu.SMEM)


def ring_routes(devices):
    chips = devices // 2
    cycle = list(range(0, chips, 2)) + list(range(1, chips, 2))[::-1]
    onward, backward = [], []
    for place, chip in enumerate(cycle):
        following = cycle[(place + 1) % chips]
        for core in range(2):
            onward.append((chip * 2 + core, following * 2 + core))
            backward.append((following * 2 + core, chip * 2 + core))
    partner = [(device, device ^ 1) for device in range(devices)]
    return onward, backward, partner


def send(block, route):
    return lax.ppermute(block, AXIS, route)


def tie(*arrays):
    return lax.optimization_barrier(arrays)


def call(kernel, name, core, outs, scratch, flops, operands, from_hbm=()):
    limit = 6 * MIB + sum(4 * shape[0] * shape[1] for shape in scratch)
    semaphores = [pltpu.SemaphoreType.DMA((1,))] if from_hbm else []
    return pl.pallas_call(
        kernel,
        in_specs=[IN_SMEM]
        + [IN_VMEM] * len(operands)
        + [pl.BlockSpec(memory_space=pltpu.HBM)] * len(from_hbm),
        out_specs=[IN_VMEM] * len(outs),
        out_shape=[pltpu.VMEM(shape, kind) for shape, kind in outs],
        scratch_shapes=[pltpu.VMEM(shape, F32) for shape in scratch] + semaphores,
        compiler_params=pltpu.CompilerParams(vmem_limit_bytes=limit),
        cost_estimate=pl.CostEstimate(
            flops=flops, bytes_accessed=sum(x.size * 2 for x in operands), transcendentals=0
        ),
        name=name,
    )(core, *[in_vmem(x) for x in operands], *[in_hbm(x) for x in from_hbm])


def in_hbm(x):
    return pltpu.with_memory_space_constraint(x, pltpu.HBM)


def in_vmem(x):
    return pltpu.with_memory_space_constraint(x, pltpu.VMEM)


def fetch(weights, after):
    count = len(weights)

    def kernel(after_ref, *refs):
        copies = [
            pltpu.make_async_copy(refs[i], refs[count + i], refs[-1].at[i]) for i in range(count)
        ]
        for copy in copies:
            copy.start()
        for copy in copies:
            copy.wait()

    return pl.pallas_call(
        kernel,
        in_specs=[pl.BlockSpec(memory_space=pl.ANY)] + [pl.BlockSpec(memory_space=pltpu.HBM)] * count,
        out_specs=[IN_VMEM] * count,
        out_shape=[pltpu.VMEM(w.shape, w.dtype) for w in weights],
        scratch_shapes=[pltpu.SemaphoreType.DMA((count,))],
        compiler_params=pltpu.CompilerParams(vmem_limit_bytes=MIB),
        cost_estimate=pl.CostEstimate(
            flops=0, bytes_accessed=sum(2 * w.size for w in weights), transcendentals=0
        ),
        name="fetch",
    )(after, *[in_hbm(w) for w in weights])


def passes(core, half, tile):
    for own in (True, False):
        start = (core if own else 1 - core) * half
        for k in range(0, half, tile):
            yield own, slice(k, k + tile), pl.ds(pl.multiple_of(start + k, tile), tile)


def forward_own(core, same, weights):
    count = len(same)
    total = sum(b.shape[0] for b in same)
    depth, columns = weights[0].shape

    def kernel(core_ref, *refs):
        blocks, weight_refs, sums = refs[:count], refs[count : count + 3], refs[count + 3 :]
        for own, near, at in passes(core_ref[0], depth // 2, 1024):
            if own:
                left = jnp.concatenate([b[:, near] for b in blocks])
                for s, w in zip(sums, weight_refs):
                    product = jnp.dot(left, w[at, :], preferred_element_type=F32)
                    if near.start == 0:
                        s[...] = product
                    else:
                        s[...] += product

    return call(
        kernel,
        "forward_own",
        core,
        [((total, columns), F32)] * 3,
        [],
        3 * total * depth * columns,
        [*same, *weights],
    )


def forward(core, same, other, weights, late=None, beside=None, begun=()):
    count, rows = len(other), other[0].shape[0]
    same = [] if begun else same
    first = len(same)
    total = count * rows
    depth, columns = weights[0].shape
    known = len(weights)
    coming = [w for w in (late, beside) if w is not None]

    def kernel(core_ref, *refs):
        blocks, refs = refs[: first + count], refs[first + count :]
        weight_refs, refs = list(refs[:known]), refs[known:]
        begun_refs, refs = refs[: len(begun)], refs[len(begun) :]
        source, refs = refs[: len(coming)], refs[len(coming) :]
        (hidden_ref, by_dot_ref, by_error_ref), refs = refs[:3], refs[3:]
        arriving, refs = refs[: len(coming)], refs[len(coming) :]
        sums = refs[:3]
        if coming:
            copy = pltpu.make_async_copy(source[0], arriving[0], refs[3].at[0])
            copy.start()
            if late is not None:
                weight_refs.append(arriving[0])

        def add(some):
            for own, near, at in passes(core_ref[0], depth // 2, 1024):
                part = blocks[:first] if own else blocks[first:]
                if not part:
                    continue
                left = jnp.concatenate([b[:, near] for b in part])
                for n, (s, w) in enumerate(some):
                    product = jnp.dot(left, w[at, :], preferred_element_type=F32)
                    if begun and near.start == 0:
                        s[...] = begun_refs[n][...] + product
                    elif own and near.start == 0:
                        s[...] = product
                    else:
                        s[...] += product

        pairs = list(zip(sums, weight_refs))
        add(pairs[:known])
        if coming:
            copy.wait()
        if late is not None:
            add(pairs[known:])
        for b in range(count):
            at = slice(b * rows, (b + 1) * rows)
            preact, linear = sums[0][at, :], sums[1][at, :]
            tangent = sums[2][at, :] * depth ** (-0.5)
            logistic = jax.nn.sigmoid(preact)
            slopes = logistic * (1.0 + preact * (1.0 - logistic))
            curvature = logistic * (1.0 - logistic) * (2.0 + preact * (1.0 - 2.0 * logistic))
            by_dot = linear * slopes
            by_dot_ref[at, :] = by_dot
            by_error_ref[at, :] = linear * curvature * tangent
            hidden_ref[2 * b * rows : (2 * b + 1) * rows, :] = (preact * logistic * linear).astype(BF16)
            hidden_ref[(2 * b + 1) * rows : (2 * b + 2) * rows, :] = (by_dot * tangent).astype(BF16)

    return call(
        kernel,
        "forward",
        core,
        [((2 * total, columns), BF16), ((total, columns), F32), ((total, columns), F32)]
        + [(w.shape, w.dtype) for w in coming],
        [(total, columns)] * 3,
        (3 if begun else 6) * total * depth * columns,
        [*same, *other, *weights, *begun],
        coming,
    )


def down(core, hidden, down_weight, both=True, own_half=True):
    total = sum(h.shape[0] for h in hidden)
    depth, columns = down_weight.shape
    half = columns // 2
    places = 2 if both else 1

    def kernel(core_ref, *refs):
        hidden_refs, weight_ref, out_refs = refs[: len(hidden)], refs[len(hidden)], refs[len(hidden) + 1 :]
        left = jnp.concatenate([h[...] for h in hidden_refs])
        first = core_ref[0] if own_half and not both else 1 - core_ref[0]
        for mine, near, at in passes(first, half, 1024):
            if mine or both:
                product = jnp.dot(left, weight_ref[:, at], preferred_element_type=F32)
                out_refs[0 if mine else 1][:, near] = product.astype(BF16)

    return call(
        kernel,
        "down",
        core,
        [((total, half), BF16)] * places,
        [],
        places * total * depth * columns,
        [*hidden, down_weight],
    )


def merge(core, sums, shape, splits=1, under=False):
    rows, columns = shape
    arrays = []
    plan = []
    for terms in sums:
        places = []
        for array, *rest in terms:
            known = [n for n, x in enumerate(arrays) if x is array]
            if not known:
                arrays.append(array)
            places.append((known[0] if known else len(arrays) - 1, *rest))
        plan.append(places)
    piece = columns // splits

    def kernel(core_ref, *refs):
        out_refs = refs[len(arrays) :]
        for n, places in enumerate(plan):
            for start in range(0, columns, columns // 4):
                width = columns // 4
                value = None
                for at, row, column, *sign in places:
                    if start < column or start >= column + arrays[at].shape[1]:
                        continue
                    term = refs[at][row : row + rows, start - column : start - column + width].astype(F32)
                    if value is None:
                        value = term
                    else:
                        value = value - term if sign else value + term
                out = out_refs[0 if under else n * splits + start // piece]
                at = n * rows if under else 0
                out[at : at + rows, start % piece : start % piece + width] = value.astype(BF16)

    outs = [((len(sums) * rows, columns), BF16)]
    if not under:
        outs = [((rows, piece), BF16)] * (len(sums) * splits)
    return call(kernel, "merge", core, outs, [], 0, arrays)


def stack(core, sums, shape):
    return merge(core, sums, (shape[0] // len(sums), shape[1]), under=True)[0]


def back_own(core, same, down_weight):
    total = sum(b.shape[0] for b in same)
    columns, depth = down_weight.shape

    def kernel(core_ref, *refs):
        blocks, weight_ref, sum_ref = refs[:-2], refs[-2], refs[-1]
        for own, near, at in passes(core_ref[0], depth // 2, 1024):
            if own:
                left = jnp.concatenate([b[:, near] for b in blocks])
                product = lax.dot_general(
                    left, weight_ref[:, at], (((1,), (1,)), ((), ())), preferred_element_type=F32
                )
                if near.start == 0:
                    sum_ref[...] = product
                else:
                    sum_ref[...] += product

    return call(
        kernel,
        "back_own",
        core,
        [((total, columns), F32)],
        [],
        total * depth * columns,
        [*same, down_weight],
    )


def back(core, same, other, down_weight, by_dot, by_error, begun=()):
    count, rows = len(other), other[0].shape[0]
    total = count * rows
    same = [] if begun else same
    first = len(same)
    columns, depth = down_weight.shape
    parts = len(by_dot)

    def kernel(core_ref, *refs):
        blocks, refs = refs[: first + count], refs[first + count :]
        begun_refs, refs = refs[: len(begun)], refs[len(begun) :]
        weight_ref, by_dot_refs, by_error_refs = refs[0], refs[1 : 1 + parts], refs[1 + parts : -2]
        out_ref, sum_ref = refs[-2:]
        for own, near, at in passes(core_ref[0], depth // 2, 1024):
            part = blocks[:first] if own else blocks[first:]
            if not part:
                continue
            left = jnp.concatenate([b[:, near] for b in part])
            product = lax.dot_general(
                left, weight_ref[:, at], (((1,), (1,)), ((), ())), preferred_element_type=F32
            )
            if begun and near.start == 0:
                sum_ref[...] = begun_refs[0][...] + product
            elif own and near.start == 0:
                sum_ref[...] = product
            else:
                sum_ref[...] += product
        half = rows // 2
        b = 0
        for by_dot_ref, by_error_ref in zip(by_dot_refs, by_error_refs):
            for start in range(0, by_dot_ref.shape[0], half):
                at = slice(start, start + half)
                gradient = sum_ref[b * rows : b * rows + half, :]
                gradient_dot = sum_ref[b * rows + half : (b + 1) * rows, :]
                out_ref[b * half : (b + 1) * half, :] = (
                    gradient_dot * by_dot_ref[at, :] + gradient * by_error_ref[at, :]
                ).astype(BF16)
                b += 1

    return call(
        kernel,
        "back",
        core,
        [((total // 2, columns), BF16)],
        [(total, columns)],
        (1 if begun else 2) * total * depth * columns,
        [*same, *other, *begun, down_weight, *by_dot, *by_error],
    )[0]


def outer(core, same, other, weighted, scale):
    count, rows = len(same), same[0].shape[0]
    half = same[0].shape[1]
    total, depth = count * rows, 2 * half
    columns = weighted[0].shape[1]
    tile = 512

    def kernel(core_ref, *refs):
        blocks, refs = refs[: 2 * count], refs[2 * count :]
        weighted_refs, (out_ref, held, sems) = refs[:-3], refs[-3:]
        right = jnp.concatenate([w[...] for w in weighted_refs])
        copies = []
        for own, near, at in passes(core_ref[0], half, tile):
            left = jnp.concatenate([b[:, near] for b in (blocks[:count] if own else blocks[count:])])
            product = lax.dot_general(
                left, right, (((0,), (0,)), ((), ())), preferred_element_type=F32
            )
            slot = len(copies)
            held[slot] = (product * scale).astype(BF16)
            copies.append(pltpu.make_async_copy(held.at[slot], out_ref.at[at], sems.at[slot]))
            copies[-1].start()
        for copy in copies:
            copy.wait()

    operands = [*same, *other, *weighted]
    tiles = depth // tile
    return pl.pallas_call(
        kernel,
        in_specs=[IN_SMEM] + [IN_VMEM] * len(operands),
        out_specs=pl.BlockSpec(memory_space=pltpu.HBM),
        out_shape=jax.ShapeDtypeStruct((depth, columns), BF16),
        scratch_shapes=[pltpu.VMEM((tiles, tile, columns), BF16), pltpu.SemaphoreType.DMA((tiles,))],
        compiler_params=pltpu.CompilerParams(vmem_limit_bytes=24 * MIB),
        cost_estimate=pl.CostEstimate(
            flops=2 * total * depth * columns, bytes_accessed=2 * depth * columns, transcendentals=0
        ),
        name="outer",
    )(core, *[in_vmem(x) for x in operands])


def on_device(devices, tokens, targets, gate_weight, up_weight, down_weight, probe):
    mine, features = tokens.shape
    rows, half, quarter = 2 * mine, features // 2, features // 4
    onward, backward, partner = ring_routes(devices)
    chips = devices // 2
    steps = (chips - 1) // 2
    count = chips
    even = chips % 2 == 0
    index = lax.rem(lax.axis_index(AXIS), 2)
    core = index.astype(jnp.int32).reshape(1)

    def chip_rows(array):
        keep = lax.dynamic_slice(array, (0, index * half), (mine, half))
        give = lax.dynamic_slice(array, (0, (1 - index) * half), (mine, half))
        got = send(give, partner)
        return jnp.where(index == 0, jnp.concatenate([keep, got]), jnp.concatenate([got, keep]))

    last = 1 + 2 * steps
    cuts = [0, max(1, last - 4), max(1, last - 2), count]
    groups = [list(range(a, b)) for a, b in zip(cuts, cuts[1:]) if a < b]

    def gather(owns, work):
        chains = range(len(owns))
        same, other = [[own] for own in owns], [[] for _ in owns]
        ends = [(own, own) for own in owns]

        def swap():
            for c in chains:
                other[c] += [send(block, partner) for block in same[c][len(other[c]) :]]

        for step in range(1, steps + 1):
            moved = [(send(ends[c][0], onward), send(ends[c][1], backward)) for c in chains]
            swap()
            done = work(step, same, other)
            for c in chains:
                before, after = moved[c]
                if done:
                    before, after = tie(before, *done)[0], tie(after, *done)[0]
                ends[c] = before, after
                same[c] += [before, after]
        if even:
            moved = [
                (send(ends[c][0][:, :quarter], onward), send(ends[c][1][:, quarter:], backward))
                for c in chains
            ]
            swap()
            done = work(steps + 1, same, other)
            for c in chains:
                near, far = moved[c]
                if done:
                    near, far = tie(near, *done)[0], tie(far, *done)[0]
                same[c].append(jnp.concatenate([near, far], axis=1))
        swap()
        work(steps + 2, same, other)
        return same, other

    hidden, by_dot, by_error = [], [], []
    weights = {}

    def run_forward(step, same, other):
        same, other = same[0], other[0]
        if step == 1:
            weights["gate"], weights["up"] = fetch([gate_weight, up_weight], same[0])
            return [weights["gate"], weights["up"]]
        done = []
        ready = len(other) if step > steps + 1 else len(other) - 2
        while len(hidden) < len(groups) and groups[len(hidden)][-1] < ready:
            g = groups[len(hidden)]
            at = slice(g[0], g[-1] + 1)
            late = None if "probe" in weights else probe
            beside = down_weight if late is None and "down" not in weights else None
            known = [weights[n] for n in ("gate", "up", "probe") if n in weights]
            begun = ()
            if step > steps + 1 and late is None:
                begun = forward_own(core, same[at], known)
            h, d, e, *came = forward(core, same[at], other[at], known, late, beside, begun)
            hidden.append(h), by_dot.append(d), by_error.append(e)
            if came:
                weights["down" if late is None else "probe"] = came[0]
            done.append(h)
            if step <= steps + 1:
                break
        return done

    (same,), (other,) = gather([chip_rows(tokens)], run_forward)
    if "down" not in weights:
        (weights["down"],) = fetch([down_weight], hidden[-1])
    goals = chip_rows(targets)

    split = max(len(groups) - 1, 1)
    near_blocks = [b for g in groups[:split] for b in g]
    far_blocks = [b for g in groups[split:] for b in g]
    partial, swapped = {}, {}

    def keep(blocks, own, others):
        for at, b in enumerate(blocks):
            at = slice(2 * rows * at, 2 * rows * (at + 1))
            partial[b] = (own, at.start)
            swapped[b] = send(others[at], partner)

    def terms_of(b, row=0):
        own, start = partial[b]
        return [(own, start + row, 0), (swapped[b], row, 0)]

    def near_work(after):
        hidden_near = tie(*hidden[:split], after)[:-1]
        others, own = down(core, hidden_near, weights["down"])
        keep(near_blocks, own, others)
        return own

    if far_blocks:
        (others,) = down(core, hidden[split:], weights["down"], both=False, own_half=False)
        (own,) = down(core, [*hidden[split:]], weights["down"], both=False)
        keep(far_blocks, own, others)
    else:
        near_work(hidden[-1])

    shape = (2 * rows, half)
    from_before = from_after = None
    if even:
        to_after, to_before = merge(core, [terms_of(count - 1)], shape, splits=2)
        from_before, from_after = send(to_after, onward), send(to_before, backward)
        if far_blocks:
            from_before, from_after, _ = tie(from_before, from_after, near_work(to_after))
    for distance in range(steps, 0, -1):
        to_after, to_before = terms_of(2 * distance), terms_of(2 * distance - 1)
        if from_before is not None:
            to_after.append((from_before, 0, 0))
            to_before.append((from_after, 0, half - from_after.shape[1]))
        if False:
            to_after, to_before = merge(core, [to_after, to_before], shape)
        else:
            (to_after,), (to_before,) = merge(core, [to_after], shape), merge(core, [to_before], shape)
        from_before, from_after = send(to_after, onward), send(to_before, backward)
        if distance == steps and not even and far_blocks:
            from_before, from_after, _ = tie(from_before, from_after, near_work(to_after))
    parts = []
    for row in (0, rows):
        terms = terms_of(0, row) + [(from_before, row, 0), (from_after, row, 0)]
        if row == 0:
            terms.append((goals, 0, 0, -1))
        parts.append(terms)
    message = stack(core, parts, shape)

    weighted = []
    back_groups = [groups[:split], *[[g] for g in groups[split:]]]

    def run_back(step, same, other):
        done = []
        ready = len(other[0])
        while len(weighted) < len(back_groups) and back_groups[len(weighted)][-1][-1] < ready:
            gs = back_groups[len(weighted)]
            at = slice(gs[0][0], gs[-1][-1] + 1)
            first = sum(len(x) for x in back_groups[: len(weighted)])
            saved = slice(first, first + len(gs))
            begun = back_own(core, same[0][at], weights["down"]) if step > steps + 1 else ()
            weighted.append(
                back(
                    core,
                    same[0][at],
                    other[0][at],
                    weights["down"],
                    by_dot[saved],
                    by_error[saved],
                    begun,
                )
            )
            done.append(weighted[-1])
        return done

    gather([message], run_back)
    return outer(core, same, other, weighted, (mine * devices) ** (-0.5))


def solution(mesh):
    placed = (
        P(("groups", "tensor"), None),
        P(("groups", "tensor"), None),
        P(None, "tensor"),
        P(None, "tensor"),
        P("tensor", None),
        P("groups", "tensor"),
    )
    return jax.shard_map(
        functools.partial(on_device, mesh.shape[AXIS]),
        mesh=mesh,
        in_specs=placed,
        out_specs=P("groups", "tensor"),
        check_vma=False,
    )
```

```python
import functools

import jax
import jax.numpy as jnp
from jax import lax
from jax.experimental import pallas as pl
from jax.experimental.pallas import tpu as pltpu
from jax.sharding import PartitionSpec as P

AXIS = "tensor"
F32, BF16 = jnp.float32, jnp.bfloat16
MIB = 2**20
IN_VMEM = pl.BlockSpec(memory_space=pltpu.VMEM)
IN_SMEM = pl.BlockSpec(memory_space=pltpu.SMEM)


def ring_routes(devices):
    chips = devices // 2
    cycle = list(range(0, chips, 2)) + list(range(1, chips, 2))[::-1]
    onward, backward = [], []
    for place, chip in enumerate(cycle):
        following = cycle[(place + 1) % chips]
        for core in range(2):
            onward.append((chip * 2 + core, following * 2 + core))
            backward.append((following * 2 + core, chip * 2 + core))
    partner = [(device, device ^ 1) for device in range(devices)]
    return onward, backward, partner


def send(block, route):
    return lax.ppermute(block, AXIS, route)


def tie(*arrays):
    return lax.optimization_barrier(arrays)


def call(kernel, name, core, outs, scratch, flops, operands, from_hbm=()):
    limit = 6 * MIB + sum(4 * shape[0] * shape[1] for shape in scratch)
    semaphores = [pltpu.SemaphoreType.DMA((1,))] if from_hbm else []
    return pl.pallas_call(
        kernel,
        in_specs=[IN_SMEM]
        + [IN_VMEM] * len(operands)
        + [pl.BlockSpec(memory_space=pltpu.HBM)] * len(from_hbm),
        out_specs=[IN_VMEM] * len(outs),
        out_shape=[pltpu.VMEM(shape, kind) for shape, kind in outs],
        scratch_shapes=[pltpu.VMEM(shape, F32) for shape in scratch] + semaphores,
        compiler_params=pltpu.CompilerParams(vmem_limit_bytes=limit),
        cost_estimate=pl.CostEstimate(
            flops=flops, bytes_accessed=sum(x.size * 2 for x in operands), transcendentals=0
        ),
        name=name,
    )(core, *[in_vmem(x) for x in operands], *[in_hbm(x) for x in from_hbm])


def in_hbm(x):
    return pltpu.with_memory_space_constraint(x, pltpu.HBM)


def in_vmem(x):
    return pltpu.with_memory_space_constraint(x, pltpu.VMEM)


def fetch(weights, after):
    count = len(weights)

    def kernel(after_ref, *refs):
        copies = [
            pltpu.make_async_copy(refs[i], refs[count + i], refs[-1].at[i]) for i in range(count)
        ]
        for copy in copies:
            copy.start()
        for copy in copies:
            copy.wait()

    return pl.pallas_call(
        kernel,
        in_specs=[pl.BlockSpec(memory_space=pl.ANY)] + [pl.BlockSpec(memory_space=pltpu.HBM)] * count,
        out_specs=[IN_VMEM] * count,
        out_shape=[pltpu.VMEM(w.shape, w.dtype) for w in weights],
        scratch_shapes=[pltpu.SemaphoreType.DMA((count,))],
        compiler_params=pltpu.CompilerParams(vmem_limit_bytes=MIB),
        cost_estimate=pl.CostEstimate(
            flops=0, bytes_accessed=sum(2 * w.size for w in weights), transcendentals=0
        ),
        name="fetch",
    )(after, *[in_hbm(w) for w in weights])


def passes(core, half, tile):
    for own in (True, False):
        start = (core if own else 1 - core) * half
        for k in range(0, half, tile):
            yield own, slice(k, k + tile), pl.ds(pl.multiple_of(start + k, tile), tile)


def forward_own(core, same, weights):
    count = len(same)
    total = sum(b.shape[0] for b in same)
    depth, columns = weights[0].shape

    def kernel(core_ref, *refs):
        blocks, weight_refs, sums = refs[:count], refs[count : count + 3], refs[count + 3 :]
        for own, near, at in passes(core_ref[0], depth // 2, 1024):
            if own:
                left = jnp.concatenate([b[:, near] for b in blocks])
                for s, w in zip(sums, weight_refs):
                    product = jnp.dot(left, w[at, :], preferred_element_type=F32)
                    if near.start == 0:
                        s[...] = product
                    else:
                        s[...] += product

    return call(
        kernel,
        "forward_own",
        core,
        [((total, columns), F32)] * 3,
        [],
        3 * total * depth * columns,
        [*same, *weights],
    )


def forward(core, same, other, weights, late=None, beside=None, begun=()):
    count, rows = len(other), other[0].shape[0]
    same = [] if begun else same
    first = len(same)
    total = count * rows
    depth, columns = weights[0].shape
    known = len(weights)
    coming = [w for w in (late, beside) if w is not None]

    def kernel(core_ref, *refs):
        blocks, refs = refs[: first + count], refs[first + count :]
        weight_refs, refs = list(refs[:known]), refs[known:]
        begun_refs, refs = refs[: len(begun)], refs[len(begun) :]
        source, refs = refs[: len(coming)], refs[len(coming) :]
        (hidden_ref, by_dot_ref, by_error_ref), refs = refs[:3], refs[3:]
        arriving, refs = refs[: len(coming)], refs[len(coming) :]
        sums = refs[:3]
        if coming:
            copy = pltpu.make_async_copy(source[0], arriving[0], refs[3].at[0])
            copy.start()
            if late is not None:
                weight_refs.append(arriving[0])

        def add(some):
            for own, near, at in passes(core_ref[0], depth // 2, 1024):
                part = blocks[:first] if own else blocks[first:]
                if not part:
                    continue
                left = jnp.concatenate([b[:, near] for b in part])
                for n, (s, w) in enumerate(some):
                    product = jnp.dot(left, w[at, :], preferred_element_type=F32)
                    if begun and near.start == 0:
                        s[...] = begun_refs[n][...] + product
                    elif own and near.start == 0:
                        s[...] = product
                    else:
                        s[...] += product

        pairs = list(zip(sums, weight_refs))
        add(pairs[:known])
        if coming:
            copy.wait()
        if late is not None:
            add(pairs[known:])
        for b in range(count):
            at = slice(b * rows, (b + 1) * rows)
            preact, linear = sums[0][at, :], sums[1][at, :]
            tangent = sums[2][at, :] * depth ** (-0.5)
            logistic = jax.nn.sigmoid(preact)
            slopes = logistic * (1.0 + preact * (1.0 - logistic))
            curvature = logistic * (1.0 - logistic) * (2.0 + preact * (1.0 - 2.0 * logistic))
            by_dot = linear * slopes
            by_dot_ref[at, :] = by_dot
            by_error_ref[at, :] = linear * curvature * tangent
            hidden_ref[2 * b * rows : (2 * b + 1) * rows, :] = (preact * logistic * linear).astype(BF16)
            hidden_ref[(2 * b + 1) * rows : (2 * b + 2) * rows, :] = (by_dot * tangent).astype(BF16)

    return call(
        kernel,
        "forward",
        core,
        [((2 * total, columns), BF16), ((total, columns), F32), ((total, columns), F32)]
        + [(w.shape, w.dtype) for w in coming],
        [(total, columns)] * 3,
        (3 if begun else 6) * total * depth * columns,
        [*same, *other, *weights, *begun],
        coming,
    )


def down(core, hidden, down_weight, both=True, own_half=True):
    total = sum(h.shape[0] for h in hidden)
    depth, columns = down_weight.shape
    half = columns // 2
    places = 2 if both else 1

    def kernel(core_ref, *refs):
        hidden_refs, weight_ref, out_refs = refs[: len(hidden)], refs[len(hidden)], refs[len(hidden) + 1 :]
        left = jnp.concatenate([h[...] for h in hidden_refs])
        first = core_ref[0] if own_half and not both else 1 - core_ref[0]
        for mine, near, at in passes(first, half, 1024):
            if mine or both:
                product = jnp.dot(left, weight_ref[:, at], preferred_element_type=F32)
                out_refs[0 if mine else 1][:, near] = product.astype(BF16)

    return call(
        kernel,
        "down",
        core,
        [((total, half), BF16)] * places,
        [],
        places * total * depth * columns,
        [*hidden, down_weight],
    )


def merge(core, sums, shape, splits=1, under=False):
    rows, columns = shape
    arrays = []
    plan = []
    for terms in sums:
        places = []
        for array, *rest in terms:
            known = [n for n, x in enumerate(arrays) if x is array]
            if not known:
                arrays.append(array)
            places.append((known[0] if known else len(arrays) - 1, *rest))
        plan.append(places)
    piece = columns // splits

    def kernel(core_ref, *refs):
        out_refs = refs[len(arrays) :]
        for n, places in enumerate(plan):
            for start in range(0, columns, columns // 4):
                width = columns // 4
                value = None
                for at, row, column, *sign in places:
                    if start < column or start >= column + arrays[at].shape[1]:
                        continue
                    term = refs[at][row : row + rows, start - column : start - column + width].astype(F32)
                    if value is None:
                        value = term
                    else:
                        value = value - term if sign else value + term
                out = out_refs[0 if under else n * splits + start // piece]
                at = n * rows if under else 0
                out[at : at + rows, start % piece : start % piece + width] = value.astype(BF16)

    outs = [((len(sums) * rows, columns), BF16)]
    if not under:
        outs = [((rows, piece), BF16)] * (len(sums) * splits)
    return call(kernel, "merge", core, outs, [], 0, arrays)


def stack(core, sums, shape):
    return merge(core, sums, (shape[0] // len(sums), shape[1]), under=True)[0]


def back_own(core, same, down_weight):
    total = sum(b.shape[0] for b in same)
    columns, depth = down_weight.shape

    def kernel(core_ref, *refs):
        blocks, weight_ref, sum_ref = refs[:-2], refs[-2], refs[-1]
        for own, near, at in passes(core_ref[0], depth // 2, 1024):
            if own:
                left = jnp.concatenate([b[:, near] for b in blocks])
                product = lax.dot_general(
                    left, weight_ref[:, at], (((1,), (1,)), ((), ())), preferred_element_type=F32
                )
                if near.start == 0:
                    sum_ref[...] = product
                else:
                    sum_ref[...] += product

    return call(
        kernel,
        "back_own",
        core,
        [((total, columns), F32)],
        [],
        total * depth * columns,
        [*same, down_weight],
    )


def back(core, same, other, down_weight, by_dot, by_error, begun=()):
    count, rows = len(other), other[0].shape[0]
    total = count * rows
    same = [] if begun else same
    first = len(same)
    columns, depth = down_weight.shape
    parts = len(by_dot)

    def kernel(core_ref, *refs):
        blocks, refs = refs[: first + count], refs[first + count :]
        begun_refs, refs = refs[: len(begun)], refs[len(begun) :]
        weight_ref, by_dot_refs, by_error_refs = refs[0], refs[1 : 1 + parts], refs[1 + parts : -2]
        out_ref, sum_ref = refs[-2:]
        for own, near, at in passes(core_ref[0], depth // 2, 1024):
            part = blocks[:first] if own else blocks[first:]
            if not part:
                continue
            left = jnp.concatenate([b[:, near] for b in part])
            product = lax.dot_general(
                left, weight_ref[:, at], (((1,), (1,)), ((), ())), preferred_element_type=F32
            )
            if begun and near.start == 0:
                sum_ref[...] = begun_refs[0][...] + product
            elif own and near.start == 0:
                sum_ref[...] = product
            else:
                sum_ref[...] += product
        half = rows // 2
        b = 0
        for by_dot_ref, by_error_ref in zip(by_dot_refs, by_error_refs):
            for start in range(0, by_dot_ref.shape[0], half):
                at = slice(start, start + half)
                gradient = sum_ref[b * rows : b * rows + half, :]
                gradient_dot = sum_ref[b * rows + half : (b + 1) * rows, :]
                out_ref[b * half : (b + 1) * half, :] = (
                    gradient_dot * by_dot_ref[at, :] + gradient * by_error_ref[at, :]
                ).astype(BF16)
                b += 1

    return call(
        kernel,
        "back",
        core,
        [((total // 2, columns), BF16)],
        [(total, columns)],
        (1 if begun else 2) * total * depth * columns,
        [*same, *other, *begun, down_weight, *by_dot, *by_error],
    )[0]


def turn(core, same, other):
    half = same[0].shape[1]
    total = sum(b.shape[0] for b in same)

    def kernel(core_ref, *refs):
        blocks, out_ref = refs[:-1], refs[-1]
        for n, part in enumerate((blocks[: len(same)], blocks[len(same) :])):
            for start in range(0, half, 512):
                left = jnp.concatenate([b[:, start : start + 512] for b in part])
                out_ref[n * half + start : n * half + start + 512, :] = left.T

    return call(kernel, "turn", core, [((2 * half, total), BF16)], [], 0, [*same, *other])[0]


def outer(core, turned, weighted, scale):
    depth, total = turned.shape
    half = depth // 2
    columns = weighted[0].shape[1]
    tile = 512

    def kernel(core_ref, *refs):
        turned_ref, weighted_refs, (out_ref, held, sems) = refs[0], refs[1:-3], refs[-3:]
        right = jnp.concatenate([w[...] for w in weighted_refs])
        copies = []
        for own, near, at in passes(core_ref[0], half, tile):
            first = near.start + (0 if own else half)
            product = jnp.dot(turned_ref[first : first + tile, :], right, preferred_element_type=F32)
            slot = len(copies)
            held[slot] = (product * scale).astype(BF16)
            copies.append(pltpu.make_async_copy(held.at[slot], out_ref.at[at], sems.at[slot]))
            copies[-1].start()
        for copy in copies:
            copy.wait()

    operands = [turned, *weighted]
    tiles = depth // tile
    return pl.pallas_call(
        kernel,
        in_specs=[IN_SMEM] + [IN_VMEM] * len(operands),
        out_specs=pl.BlockSpec(memory_space=pltpu.HBM),
        out_shape=jax.ShapeDtypeStruct((depth, columns), BF16),
        scratch_shapes=[pltpu.VMEM((tiles, tile, columns), BF16), pltpu.SemaphoreType.DMA((tiles,))],
        compiler_params=pltpu.CompilerParams(vmem_limit_bytes=24 * MIB),
        cost_estimate=pl.CostEstimate(
            flops=2 * total * depth * columns, bytes_accessed=2 * depth * columns, transcendentals=0
        ),
        name="outer",
    )(core, *[in_vmem(x) for x in operands])


def on_device(devices, tokens, targets, gate_weight, up_weight, down_weight, probe):
    mine, features = tokens.shape
    rows, half, quarter = 2 * mine, features // 2, features // 4
    onward, backward, partner = ring_routes(devices)
    chips = devices // 2
    steps = (chips - 1) // 2
    count = chips
    even = chips % 2 == 0
    index = lax.rem(lax.axis_index(AXIS), 2)
    core = index.astype(jnp.int32).reshape(1)

    def chip_rows(array):
        keep = lax.dynamic_slice(array, (0, index * half), (mine, half))
        give = lax.dynamic_slice(array, (0, (1 - index) * half), (mine, half))
        got = send(give, partner)
        return jnp.where(index == 0, jnp.concatenate([keep, got]), jnp.concatenate([got, keep]))

    last = 1 + 2 * steps
    cuts = [0, max(1, last - 4), max(1, last - 2), count]
    groups = [list(range(a, b)) for a, b in zip(cuts, cuts[1:]) if a < b]

    def gather(owns, work):
        chains = range(len(owns))
        same, other = [[own] for own in owns], [[] for _ in owns]
        ends = [(own, own) for own in owns]

        def swap():
            for c in chains:
                other[c] += [send(block, partner) for block in same[c][len(other[c]) :]]

        for step in range(1, steps + 1):
            moved = [(send(ends[c][0], onward), send(ends[c][1], backward)) for c in chains]
            swap()
            done = work(step, same, other)
            for c in chains:
                before, after = moved[c]
                if done:
                    before, after = tie(before, *done)[0], tie(after, *done)[0]
                ends[c] = before, after
                same[c] += [before, after]
        if even:
            moved = [
                (send(ends[c][0][:, :quarter], onward), send(ends[c][1][:, quarter:], backward))
                for c in chains
            ]
            swap()
            done = work(steps + 1, same, other)
            for c in chains:
                near, far = moved[c]
                if done:
                    near, far = tie(near, *done)[0], tie(far, *done)[0]
                same[c].append(jnp.concatenate([near, far], axis=1))
        swap()
        work(steps + 2, same, other)
        return same, other

    hidden, by_dot, by_error = [], [], []
    weights = {}

    def run_forward(step, same, other):
        same, other = same[0], other[0]
        if step == 1:
            weights["gate"], weights["up"] = fetch([gate_weight, up_weight], same[0])
            return [weights["gate"], weights["up"]]
        done = []
        ready = len(other) if step > steps + 1 else len(other) - 2
        while len(hidden) < len(groups) and groups[len(hidden)][-1] < ready:
            g = groups[len(hidden)]
            at = slice(g[0], g[-1] + 1)
            late = None if "probe" in weights else probe
            beside = down_weight if late is None and "down" not in weights else None
            known = [weights[n] for n in ("gate", "up", "probe") if n in weights]
            begun = ()
            if step > steps + 1 and late is None:
                begun = forward_own(core, same[at], known)
            h, d, e, *came = forward(core, same[at], other[at], known, late, beside, begun)
            hidden.append(h), by_dot.append(d), by_error.append(e)
            if came:
                weights["down" if late is None else "probe"] = came[0]
            done.append(h)
            if step <= steps + 1:
                break
        return done

    (same,), (other,) = gather([chip_rows(tokens)], run_forward)
    if "down" not in weights:
        (weights["down"],) = fetch([down_weight], hidden[-1])
    goals = chip_rows(targets)

    split = max(len(groups) - 1, 1)
    near_blocks = [b for g in groups[:split] for b in g]
    far_blocks = [b for g in groups[split:] for b in g]
    partial, swapped = {}, {}

    def keep(blocks, own, others):
        for at, b in enumerate(blocks):
            at = slice(2 * rows * at, 2 * rows * (at + 1))
            partial[b] = (own, at.start)
            swapped[b] = send(others[at], partner)

    def terms_of(b, row=0):
        own, start = partial[b]
        return [(own, start + row, 0), (swapped[b], row, 0)]

    def near_work(after):
        hidden_near = tie(*hidden[:split], after)[:-1]
        others, own = down(core, hidden_near, weights["down"])
        keep(near_blocks, own, others)
        return own

    if far_blocks:
        (others,) = down(core, hidden[split:], weights["down"], both=False, own_half=False)
        (own,) = down(core, [*hidden[split:]], weights["down"], both=False)
        keep(far_blocks, own, others)
    else:
        near_work(hidden[-1])

    shape = (2 * rows, half)
    from_before = from_after = None
    if even:
        to_after, to_before = merge(core, [terms_of(count - 1)], shape, splits=2)
        from_before, from_after = send(to_after, onward), send(to_before, backward)
        if far_blocks:
            from_before, from_after, _ = tie(from_before, from_after, near_work(to_after))
    for distance in range(steps, 0, -1):
        to_after, to_before = terms_of(2 * distance), terms_of(2 * distance - 1)
        if from_before is not None:
            to_after.append((from_before, 0, 0))
            to_before.append((from_after, 0, half - from_after.shape[1]))
        if False:
            to_after, to_before = merge(core, [to_after, to_before], shape)
        else:
            (to_after,), (to_before,) = merge(core, [to_after], shape), merge(core, [to_before], shape)
        from_before, from_after = send(to_after, onward), send(to_before, backward)
        if distance == 1:
            turned = turn(core, [tie(same[0], to_after)[0], *same[1:]], other)
            from_before, from_after = tie(from_before, turned)[0], tie(from_after, turned)[0]
        if distance == steps and not even and far_blocks:
            from_before, from_after, _ = tie(from_before, from_after, near_work(to_after))
    parts = []
    for row in (0, rows):
        terms = terms_of(0, row) + [(from_before, row, 0), (from_after, row, 0)]
        if row == 0:
            terms.append((goals, 0, 0, -1))
        parts.append(terms)
    message = stack(core, parts, shape)

    weighted = []
    back_groups = [groups[:split], *[[g] for g in groups[split:]]]

    def run_back(step, same, other):
        done = []
        ready = len(other[0])
        while len(weighted) < len(back_groups) and back_groups[len(weighted)][-1][-1] < ready:
            gs = back_groups[len(weighted)]
            at = slice(gs[0][0], gs[-1][-1] + 1)
            first = sum(len(x) for x in back_groups[: len(weighted)])
            saved = slice(first, first + len(gs))
            begun = back_own(core, same[0][at], weights["down"]) if step > steps + 1 else ()
            weighted.append(
                back(
                    core,
                    same[0][at],
                    other[0][at],
                    weights["down"],
                    by_dot[saved],
                    by_error[saved],
                    begun,
                )
            )
            done.append(weighted[-1])
        return done

    gather([message], run_back)
    return outer(core, turned, weighted, (mine * devices) ** (-0.5))


def solution(mesh):
    placed = (
        P(("groups", "tensor"), None),
        P(("groups", "tensor"), None),
        P(None, "tensor"),
        P(None, "tensor"),
        P("tensor", None),
        P("groups", "tensor"),
    )
    return jax.shard_map(
        functools.partial(on_device, mesh.shape[AXIS]),
        mesh=mesh,
        in_specs=placed,
        out_specs=P("groups", "tensor"),
        check_vma=False,
    )
```
